32 devices in a mesh: dp: 2 (over y), ctx: 16 (over z, x, core).
Axes of the slice: x: 2, y: 2, z: 4, core: 2. Of those that a mesh axis runs over, the one named last changes fastest.
Arguments:
- query_rows: bfloat16 [32768, 1024], P(('dp', 'ctx')), parts along dimension 0, may hold values from -6 to 6
- key_rows: bfloat16 [32768, 1024], P(('dp', 'ctx')), parts along dimension 0, may hold values from -6 to 6
- value_rows: bfloat16 [32768, 1024], P(('dp', 'ctx')), parts along dimension 0, may hold values from -6 to 6
- lengths: int32 [64], P('dp'), parts along dimension 0, may hold values from 1 to 10240, as said below
- conv_weight: float32 [3, 4, 1024], replicated, may hold values from -3 to 3
- out_gain: float32 [1024], replicated, may hold values from 0.1 to 1.9
Outputs:
- mixed: bfloat16 [32768, 1024], P(('dp', 'ctx')), parts along dimension 0
The draws below stay inside these ranges and needn't reach their ends.
There are 2 independent parts, one for each index of `dp`. The reference program is written for one: setup_inputs(seed, part) draws one part's arguments, and reference() takes and returns one part's arrays. A program takes and returns all parts, laid end to end along the dimension named above; an argument that names none is the same for every part. Nothing has to cross between parts.
Inputs may be any that keep to these rules, and one draw needn't show every extreme that they name: The lengths of one part sum to 16384; the last document has exactly 10240 tokens.
All inputs are finite; a program needn't handle non-finite values.
Results may differ from the reference program's by a relative error of at most 0.0065.
Values may be sent and summed in bfloat16 or wider, within the bound.
A program may use at most 128 MiB of HBM per device.

```python
import jax
import jax.numpy as jnp
from jax import lax

HEADS = 8
HEAD = 128
TOK_DEV = 1024
TOKENS = 16384
MOST = 10240
NDOC = 32
N_CTX = 16


def draw_lengths(key, part):
    rest = TOKENS - MOST
    half = MOST // 2
    points = jnp.arange(1, rest, dtype=jnp.int32)
    ranks = jax.random.permutation(jax.random.fold_in(key, 11), rest - 1).astype(jnp.int32)
    forced = points % half == 0
    ranks = jnp.where(forced, -1 - points, ranks)
    order = jnp.argsort(ranks, stable=True)
    chosen = jnp.sort(points[order[:NDOC - 2]])
    bounds = jnp.concatenate([jnp.zeros((1,), jnp.int32), chosen, jnp.full((1,), rest, jnp.int32)])
    pieces = bounds[1:] - bounds[:-1]
    return jnp.concatenate([pieces, jnp.full((1,), MOST, jnp.int32)]).astype(jnp.int32)


def levels(key, extent, split, low, top_value):
    def one(dim, shards_of):
        steps = jax.random.uniform(jax.random.fold_in(jax.random.fold_in(key, 6), dim), (shards_of,), jnp.float32, low / len(split), top_value / len(split))
        return jnp.repeat(jnp.exp(steps), extent[dim] // shards_of).reshape((-1,) + (1,) * (len(extent) - dim - 1))

    level = one(*split[0])
    for cut in split[1:]:
        level = level * one(*cut)
    return level


def gaussian(own_key, extent, deviation, limit, shards=(), kind=jnp.bfloat16):
    gain = levels(own_key, extent, shards, -0.22, 0.18) if shards else 1.0
    array = jax.random.normal(own_key, extent, jnp.float32) * deviation * gain
    return jnp.minimum(jnp.maximum(array, -limit), limit).astype(kind)


def setup_inputs(seed: int = 0, part: int = 0) -> dict:
    splits = jax.random.split(jax.random.key(seed), 7)
    own_keys = jax.random.split(jax.random.fold_in(splits[6], part), 7)
    query_rows = gaussian(own_keys[0], (TOKENS, HEADS * HEAD), 1.0, 6.0, ((0, 16),))
    key_rows = gaussian(own_keys[1], (TOKENS, HEADS * HEAD), 1.0, 6.0, ((0, 16),))
    value_rows = gaussian(own_keys[2], (TOKENS, HEADS * HEAD), 1.0, 6.0, ((0, 16),))
    lengths = draw_lengths(jax.random.fold_in(jax.random.fold_in(splits[6], part), 71), part)
    conv_weight = gaussian(splits[4], (3, 4, HEADS * HEAD), 0.5, 3.0, (), jnp.float32)
    out_gain = jnp.clip(1.0 + 0.18 * jax.random.normal(splits[5], (HEADS * HEAD,), jnp.float32), 0.1, 1.9)
    return {"query_rows": query_rows, "key_rows": key_rows, "value_rows": value_rows, "lengths": lengths, "conv_weight": conv_weight, "out_gain": out_gain}


def doc_lookup(starts, positions):
    return lax.optimization_barrier(jnp.sum((starts[None, :] <= positions[:, None]).astype(jnp.int32), axis=1)) - 1

def features(extended, doc_ext, conv_weight, row_count):
    made = []
    for which in range(3):
        summed = jnp.zeros((row_count, extended[which].shape[1]), jnp.float32)
        for delay in range(4):
            same_doc = (doc_ext[3 - delay:3 - delay + row_count] == doc_ext[3:]).astype(jnp.float32)
            shifted = extended[which][3 - delay:3 - delay + row_count].astype(jnp.float32)
            summed = summed + conv_weight[which, delay][None, :] * shifted * same_doc[:, None]
        made.append(summed)
    return (jax.nn.silu(made[0]).astype(jnp.bfloat16), jax.nn.silu(made[1]).astype(jnp.bfloat16), made[2].astype(jnp.bfloat16))

def mix_block(query_part, key_part, value_part, state_bf, use_in, doc_ids, out_gain):
    row_count = query_part.shape[0]
    block = min(512, row_count)
    pieces = []
    for block_id in range(row_count // block):
        opening = block_id * block
        closing = opening + block
        scores = jnp.einsum('qhd,khd->hqk', query_part[opening:closing].astype(jnp.float32), key_part[:closing].astype(jnp.float32))
        row_ids = jnp.arange(opening, closing)
        col_ids = jnp.arange(closing)
        allowed = (col_ids[None, :] <= row_ids[:, None]) & (doc_ids[:closing][None, :] == doc_ids[opening:closing][:, None])
        weights = jnp.where(allowed[None], scores, 0.0).astype(jnp.bfloat16)
        within = jnp.einsum('hqk,khe->qhe', weights.astype(jnp.float32), value_part[:closing].astype(jnp.float32))
        carried = jnp.einsum('qhd,hde->qhe', query_part[opening:closing].astype(jnp.float32), state_bf.astype(jnp.float32))
        pieces.append(within + carried * use_in[opening:closing, None, None])
    mixture = jnp.concatenate(pieces, axis=0)
    inverse_rms = lax.rsqrt(lax.optimization_barrier(jnp.mean(mixture * mixture, axis=-1, keepdims=True)) + 1e-06)
    normed = (mixture * inverse_rms).reshape(row_count, -1)
    return (normed * out_gain[None, :]).astype(jnp.bfloat16)

def reference(query_rows, key_rows, value_rows, lengths, conv_weight, out_gain):
    channels = query_rows.shape[1]
    starts = jnp.cumsum(lengths) - lengths
    padded = [jnp.pad(arr, ((3, 0), (0, 0))) for arr in (query_rows, key_rows, value_rows)]

    def advance(carried, device):
        offset = (device * TOK_DEV).astype(jnp.int32)
        positions = offset - 3 + jnp.arange(TOK_DEV + 3, dtype=jnp.int32)
        doc_ext = doc_lookup(starts, positions)
        extended = [lax.dynamic_slice_in_dim(arr, offset, TOK_DEV + 3, 0) for arr in padded]
        phi_q, phi_k, val = features(extended, doc_ext, conv_weight, TOK_DEV)
        doc_ids = doc_ext[3:]
        phi_q = phi_q.reshape(TOK_DEV, HEADS, HEAD)
        phi_k = phi_k.reshape(TOK_DEV, HEADS, HEAD)
        val = val.reshape(TOK_DEV, HEADS, HEAD)
        opens_here = jnp.any(starts == offset)
        use_in = ((doc_ids == doc_ids[0]) & jnp.logical_not(opens_here)).astype(jnp.float32)
        output = mix_block(phi_q, phi_k, val, carried.astype(jnp.bfloat16), use_in, doc_ids, out_gain)
        tail_mask = (doc_ids == doc_ids[-1]).astype(jnp.float32)
        tail_state = jnp.einsum('thd,the->hde', phi_k.astype(jnp.float32) * tail_mask[:, None, None], val.astype(jnp.float32))
        restart = jnp.any((starts >= offset) & (starts < offset + TOK_DEV))
        return (jnp.where(restart, tail_state, carried + tail_state), output)
    initial = jnp.zeros((HEADS, HEAD, HEAD), jnp.float32)
    _, outputs = lax.scan(advance, initial, jnp.arange(N_CTX, dtype=jnp.int32))
    return outputs.reshape(TOKENS, channels)
```

```python
import functools

import jax
import jax.numpy as jnp
from jax import lax
from jax.experimental import pallas as pl
from jax.experimental.pallas import tpu as pltpu
from jax.sharding import PartitionSpec as P

HEAD = 128
PAD = 16
MESH = pl.DeviceIdType.MESH
F32 = jnp.float32
BF16 = jnp.bfloat16


def lanes(head):
    return pl.ds(pl.multiple_of(head * HEAD, HEAD), HEAD)


def iota(shape, dim):
    return lax.broadcasted_iota(jnp.int32, shape, dim).astype(F32)


def kernel(
    n, q_hbm, k_hbm, v_hbm, len_ref, cw_ref, gain_ref, out_ref,
    rows_in, phi, mix, masks, allow, tail, gathered, scanned, carried,
    load_sem, halo_send, halo_recv, send_sem, recv_sem,
):
    me = lax.axis_index("ctx")
    T, width = q_hbm.shape
    heads = width // HEAD
    R = width // n
    ndoc = len_ref.shape[1]
    inputs = (q_hbm, k_hbm, v_hbm)

    def load(w):
        return pltpu.make_async_copy(inputs[w], rows_in.at[w, pl.ds(PAD, T)], load_sem.at[w])

    for w in (1, 2, 0):
        load(w).start()

    barrier = pltpu.get_barrier_semaphore()

    @pl.loop(1, n)
    def _(k):
        pl.semaphore_signal(
            barrier, inc=1, device_id={"ctx": lax.rem(me + k, n)}, device_id_type=MESH
        )

    sub = lax.broadcasted_iota(jnp.int32, (ndoc, ndoc), 0)
    lan = lax.broadcasted_iota(jnp.int32, (ndoc, ndoc), 1)
    lens = len_ref[...].astype(F32)
    col = jnp.sum(jnp.where(lan < sub, lens, 0.0), axis=1, keepdims=True)
    starts = jnp.sum(jnp.where(lan == sub, col, 0.0), axis=0, keepdims=True)
    offset = (me * T).astype(F32)
    end = offset + (T - 1)
    last_start = jnp.max(jnp.where(starts <= end, starts, -1.0), axis=1, keepdims=True)

    MC = 128

    @pl.loop(0, T // MC)
    def _(c):
        r0 = pl.multiple_of(c * MC, MC)
        local = (r0 + lax.broadcasted_iota(jnp.int32, (MC, 1), 0)).astype(F32)
        pos = local + offset
        mine = jnp.max(jnp.where(starts <= pos, starts, -1.0), axis=1, keepdims=True)
        depth = jnp.broadcast_to(pos - mine, (MC, HEAD))
        rows = pl.ds(r0, MC)
        for j in range(1, 4):
            masks[j - 1, rows, :] = (depth >= j).astype(F32)
        masks[3, rows, :] = (depth > local).astype(F32)
        for piece in range(T // HEAD):
            gap = local - (iota((MC, HEAD), 1) + piece * HEAD)
            ok = (gap >= 0.0) & (gap <= depth)
            allow[rows, piece * HEAD : (piece + 1) * HEAD] = jnp.where(ok, 1.0, 0.0).astype(BF16)

    C = 64

    def conv(w, c):
        r0 = pl.multiple_of(c * C, C)
        rows = pl.ds(r0, C)
        m = [masks[j, rows, :] for j in range(3)]
        for h in range(heads):
            cols = slice(h * HEAD, (h + 1) * HEAD)
            ext = rows_in[w, pl.ds(r0, C + PAD), cols].astype(F32)
            scale = 1.0 if w == 2 else 0.5
            acc = ext[PAD:] * (cw_ref[w, 0:1, cols] * scale)
            for j in range(1, 4):
                acc += (ext[PAD - j : PAD - j + C] * m[j - 1]) * (cw_ref[w, j : j + 1, cols] * scale)
            if w < 2:
                acc = acc + acc * jnp.tanh(acc)
            phi[w, rows, cols] = acc.astype(BF16)

    chunks = T // C
    half = chunks // 2

    load(1).wait()
    load(2).wait()

    @pl.loop(0, half)
    def _(i):
        conv(1, chunks - 1 - i)
        conv(2, chunks - 1 - i)

    pl.semaphore_wait(barrier, n - 1)
    nxt = lax.rem(me + 1, n)

    def halo(w):
        return pltpu.make_async_remote_copy(
            src_ref=inputs[w].at[pl.ds(T - PAD, PAD)],
            dst_ref=rows_in.at[w, pl.ds(0, PAD)],
            send_sem=halo_send.at[w],
            recv_sem=halo_recv.at[w],
            device_id={"ctx": nxt},
            device_id_type=MESH,
        )

    for w in (1, 2, 0):
        halo(w).start()

    @pl.loop(half, chunks - 1)
    def _(i):
        conv(1, chunks - 1 - i)
        conv(2, chunks - 1 - i)

    halo(1).wait_recv()
    halo(2).wait_recv()
    conv(1, 0)
    conv(2, 0)

    tail_rows = (iota((T, HEAD), 0) + offset) >= last_start

    @pl.loop(0, heads)
    def _(h):
        key = jnp.where(tail_rows, phi[1, :, lanes(h)].astype(F32), 0.0).astype(BF16)
        state = lax.dot_general(
            key, phi[2, :, lanes(h)], (((0,), (0,)), ((), ())), preferred_element_type=F32
        )
        tail[lanes(h), :] = state.astype(BF16)

    def slice_rows(d):
        return pl.ds(pl.multiple_of(d * R, R), R)

    def give(k):
        to = lax.rem(me + k, n)
        return pltpu.make_async_remote_copy(
            src_ref=tail.at[slice_rows(to)],
            dst_ref=gathered.at[slice_rows(me)],
            send_sem=send_sem.at[0, k],
            recv_sem=recv_sem.at[0, k],
            device_id={"ctx": to},
            device_id_type=MESH,
        )

    def back(k):
        to = lax.rem(me + k, n)
        return pltpu.make_async_remote_copy(
            src_ref=scanned.at[slice_rows(to)],
            dst_ref=carried.at[slice_rows(me)],
            send_sem=send_sem.at[1, k],
            recv_sem=recv_sem.at[1, k],
            device_id={"ctx": to},
            device_id_type=MESH,
        )

    @pl.loop(1, n)
    def _(k):
        give(k).start()

    gathered[slice_rows(me), :] = tail[slice_rows(me), :]

    load(0).wait()

    @pl.loop(0, chunks - 1)
    def _(i):
        conv(0, chunks - 1 - i)

    halo(0).wait_recv()
    conv(0, 0)

    B = 256

    def attend(i):
        lo, hi = i * B, (i + 1) * B

        @pl.loop(0, heads)
        def _(h):
            score = lax.dot_general(
                phi[0, lo:hi, lanes(h)], phi[1, 0:hi, lanes(h)],
                (((1,), (1,)), ((), ())), preferred_element_type=F32,
            )
            weights = score.astype(BF16) * allow[lo:hi, 0:hi]
            mix[lo:hi, lanes(h)] = jnp.dot(
                weights, phi[2, 0:hi, lanes(h)], preferred_element_type=F32
            )

    tiles = T // B
    attend(tiles - 1)

    @pl.loop(1, n)
    def _(k):
        give(k).wait_recv()

    def step(b, state):
        scanned[slice_rows(b), :] = state.astype(BF16)
        first = (b * T).astype(F32)
        inside = (starts >= first) & (starts < first + T)
        hit = jnp.max(jnp.where(inside, 1.0, 0.0), axis=1, keepdims=True)
        return state * (1.0 - hit) + gathered[slice_rows(b), :].astype(F32)

    lax.fori_loop(0, n, step, jnp.zeros((R, HEAD), F32))

    @pl.loop(1, n)
    def _(k):
        back(k).start()

    carried[slice_rows(me), :] = scanned[slice_rows(me), :]

    for i in range(tiles - 2, -1, -1):
        attend(i)

    @pl.loop(1, n)
    def _(k):
        back(k).wait_recv()

    @pl.loop(0, heads)
    def _(h):
        gain = gain_ref[:, lanes(h)]
        for i in range(tiles):
            lo, hi = i * B, (i + 1) * B
            far = jnp.dot(
                phi[0, lo:hi, lanes(h)], carried[lanes(h), :], preferred_element_type=F32
            )
            whole = mix[lo:hi, lanes(h)] + far * masks[3, lo:hi, :]
            power = jnp.mean(whole * whole, axis=1, keepdims=True)
            out_ref[lo:hi, lanes(h)] = (whole * lax.rsqrt(power + 1e-6) * gain).astype(BF16)

    for w in range(3):
        halo(w).wait_send()

    @pl.loop(1, n)
    def _(k):
        give(k).wait_send()
        back(k).wait_send()


def per_device(n, query_rows, key_rows, value_rows, lengths, conv_weight, out_gain):
    T, width = query_rows.shape
    anywhere = pl.BlockSpec(memory_space=pl.ANY)
    vmem = pl.BlockSpec(memory_space=pltpu.VMEM)
    return pl.pallas_call(
        functools.partial(kernel, n),
        out_shape=jax.ShapeDtypeStruct((T, width), BF16),
        in_specs=[anywhere] * 3 + [vmem] * 3,
        out_specs=vmem,
        scratch_shapes=[
            pltpu.VMEM((3, T + PAD, width), BF16),
            pltpu.VMEM((3, T, width), BF16),
            pltpu.VMEM((T, width), F32),
            pltpu.VMEM((4, T, HEAD), F32),
            pltpu.VMEM((T, T), BF16),
            pltpu.VMEM((width, HEAD), BF16),
            pltpu.VMEM((width, HEAD), BF16),
            pltpu.VMEM((width, HEAD), BF16),
            pltpu.VMEM((width, HEAD), BF16),
            pltpu.SemaphoreType.DMA((3,)),
            pltpu.SemaphoreType.DMA((3,)),
            pltpu.SemaphoreType.DMA((3,)),
            pltpu.SemaphoreType.DMA((2, n)),
            pltpu.SemaphoreType.DMA((2, n)),
        ],
        compiler_params=pltpu.CompilerParams(
            collective_id=0, has_side_effects=True, vmem_limit_bytes=52 * 1024 * 1024
        ),
    )(
        query_rows, key_rows, value_rows, lengths.reshape(1, -1), conv_weight,
        out_gain.reshape(1, -1),
    )


def solution(mesh):
    return jax.shard_map(
        functools.partial(per_device, mesh.shape["ctx"]),
        mesh=mesh,
        in_specs=(
            P(("dp", "ctx"), None),
            P(("dp", "ctx"), None),
            P(("dp", "ctx"), None),
            P("dp"),
            P(),
            P(),
        ),
        out_specs=P(("dp", "ctx"), None),
        check_vma=False,
    )
```

```python
import functools

import jax
import jax.numpy as jnp
from jax import lax
from jax.experimental import pallas as pl
from jax.experimental.pallas import tpu as pltpu
from jax.sharding import PartitionSpec as P

HEAD = 128
PAD = 16
B = 256
MESH = pl.DeviceIdType.MESH
F32 = jnp.float32
BF16 = jnp.bfloat16


def lanes(head):
    return pl.ds(pl.multiple_of(head * HEAD, HEAD), HEAD)


def iota(shape, dim):
    return lax.broadcasted_iota(jnp.int32, shape, dim).astype(F32)


def kernel(
    n, q_hbm, k_hbm, v_hbm, len_ref, cw_ref, mix_hbm, far_hbm, state_ref,
    rows_in, phi, mix, masks, allow, keeps, within, tail, gathered, scanned, carried,
    load_sem, halo_send, halo_recv, send_sem, recv_sem, mix_sem, far_sem,
):
    me = lax.axis_index("ctx")
    T, width = q_hbm.shape
    heads = width // HEAD
    R = width // n
    per = n // heads
    ndoc = len_ref.shape[1]
    tiles = T // B
    inputs = (q_hbm, k_hbm, v_hbm)

    def load(w):
        return pltpu.make_async_copy(inputs[w], rows_in.at[w, pl.ds(PAD, T)], load_sem.at[w])

    for w in (1, 2, 0):
        load(w).start()

    barrier = pltpu.get_barrier_semaphore()

    @pl.loop(1, n)
    def _(k):
        pl.semaphore_signal(
            barrier, inc=1, device_id={"ctx": lax.rem(me + k, n)}, device_id_type=MESH
        )

    sub = lax.broadcasted_iota(jnp.int32, (ndoc, ndoc), 0)
    lan = lax.broadcasted_iota(jnp.int32, (ndoc, ndoc), 1)
    lens = len_ref[...].astype(F32)
    col = jnp.sum(jnp.where(lan < sub, lens, 0.0), axis=1, keepdims=True)
    starts = jnp.sum(jnp.where(lan == sub, col, 0.0), axis=0, keepdims=True)
    offset = (me * T).astype(F32)

    first = iota((n, ndoc), 0) * T
    inside = (starts >= first) & (starts < first + T)
    hit = jnp.max(jnp.where(inside, 1.0, 0.0), axis=1, keepdims=True)
    keeps[...] = jnp.broadcast_to(1.0 - hit, (n, HEAD))

    MC = 128
    for c in range(T // MC):
        r0 = c * MC
        local = iota((MC, 1), 0) + r0
        pos = local + offset
        mine = jnp.max(jnp.where(starts <= pos, starts, -1.0), axis=1, keepdims=True)
        depth = jnp.broadcast_to(pos - mine, (MC, HEAD))
        rows = pl.ds(r0, MC)
        for j in range(1, 4):
            masks[j - 1, rows, :] = (depth >= j).astype(F32)
        masks[3, rows, :] = (depth > local).astype(F32)
        opening = (r0 // B) * B
        masks[4, rows, :] = (depth > local - opening).astype(F32)
        for piece in range(B // HEAD):
            gap = local - (iota((MC, HEAD), 1) + (opening + piece * HEAD))
            ok = (gap >= 0.0) & (gap <= depth)
            allow[rows, piece * HEAD : (piece + 1) * HEAD] = jnp.where(ok, 1.0, 0.0).astype(BF16)

    def last_start(c):
        end = offset + ((c + 1) * B - 1)
        return jnp.max(jnp.where(starts <= end, starts, -1.0), axis=1, keepdims=True)

    lasts = [last_start(c) - offset for c in range(tiles)]
    goes_on = [(lasts[c] < c * B).astype(F32) for c in range(tiles)]

    nxt = lax.rem(me + 1, n)

    def halo(w):
        return pltpu.make_async_remote_copy(
            src_ref=inputs[w].at[pl.ds(T - PAD, PAD)],
            dst_ref=rows_in.at[w, pl.ds(0, PAD)],
            send_sem=halo_send.at[w],
            recv_sem=halo_recv.at[w],
            device_id={"ctx": nxt},
            device_id_type=MESH,
        )

    pl.semaphore_wait(barrier, n - 1)
    for w in (1, 2, 0):
        halo(w).start()

    C = 128
    chunks = T // C

    def conv(w, h, c):
        rows = pl.ds(c * C, C)
        ext = rows_in[w, pl.ds(c * C, C + PAD), lanes(h)].astype(F32)
        scale = 1.0 if w == 2 else 0.5
        acc = ext[PAD:] * (cw_ref[w, 0:1, lanes(h)] * scale)
        for j in range(1, 4):
            tap = cw_ref[w, j : j + 1, lanes(h)] * scale
            acc += (ext[PAD - j : PAD - j + C] * masks[j - 1, rows, :]) * tap
        if w < 2:
            acc = acc + acc * jnp.tanh(acc)
        phi[w, rows, lanes(h)] = acc.astype(BF16)

    def slice_rows(d):
        return pl.ds(pl.multiple_of(d * R, R), R)

    def give(k):
        to = lax.rem(me + k, n)
        return pltpu.make_async_remote_copy(
            src_ref=tail.at[slice_rows(to)],
            dst_ref=gathered.at[slice_rows(me)],
            send_sem=send_sem.at[0, k],
            recv_sem=recv_sem.at[0, k],
            device_id={"ctx": to},
            device_id_type=MESH,
        )

    def back(k):
        to = lax.rem(me + k, n)
        return pltpu.make_async_remote_copy(
            src_ref=scanned.at[slice_rows(to)],
            dst_ref=carried.at[slice_rows(me)],
            send_sem=send_sem.at[1, k],
            recv_sem=recv_sem.at[1, k],
            device_id={"ctx": to},
            device_id_type=MESH,
        )

    def order(i):
        return lax.rem(me // per + 1 + i, heads)

    EARLY = 2
    load(1).wait()
    load(2).wait()

    @pl.loop(0, EARLY)
    def _(i):
        for c in range(chunks - 1, 0, -1):
            conv(1, order(i), c)
            conv(2, order(i), c)

    halo(1).wait_recv()
    halo(2).wait_recv()

    @pl.loop(0, heads)
    def _(i):
        h = order(i)

        @pl.when(i >= EARLY)
        def _():
            for c in range(chunks - 1, 0, -1):
                conv(1, h, c)
                conv(2, h, c)

        conv(1, h, 0)
        conv(2, h, 0)
        state = None
        for c in range(tiles):
            rows = slice(c * B, (c + 1) * B)
            live = (iota((B, HEAD), 0) + c * B) >= lasts[c]
            key = jnp.where(live, phi[1, rows, lanes(h)].astype(F32), 0.0).astype(BF16)
            own = lax.dot_general(
                key, phi[2, rows, lanes(h)], (((0,), (0,)), ((), ())), preferred_element_type=F32
            )
            state = own if state is None else state * goes_on[c] + own
            if c < tiles - 1:
                within[c, lanes(h), :] = state.astype(BF16)
        tail[lanes(h), :] = state.astype(BF16)

        @pl.loop(0, per)
        def _(j):
            k = lax.rem(h * per + j - me + n, n)

            @pl.when(k != 0)
            def _():
                give(k).start()

    gathered[slice_rows(me), :] = tail[slice_rows(me), :]

    load(0).wait()
    halo(0).wait_recv()

    def conv_q(h):
        for c in range(chunks):
            conv(0, h, c)

    pl.loop(0, heads // 2)(conv_q)

    @pl.loop(1, n)
    def _(k):
        give(k).wait_recv()

    def step(b, state):
        scanned[slice_rows(b), :] = state.astype(BF16)
        return state * keeps[pl.ds(b, 1), :] + gathered[slice_rows(b), :].astype(F32)

    lax.fori_loop(0, n, step, jnp.zeros((R, HEAD), F32), unroll=4)

    @pl.loop(1, n)
    def _(k):
        back(k).start()

    carried[slice_rows(me), :] = scanned[slice_rows(me), :]

    pl.loop(heads // 2, heads)(conv_q)

    def mix_out(i):
        rows = pl.ds(i * B, B)
        return pltpu.make_async_copy(mix.at[rows], mix_hbm.at[rows], mix_sem.at[i])

    def far_out(i):
        rows = pl.ds(i * B, B)
        return pltpu.make_async_copy(rows_in.at[0, rows], far_hbm.at[rows], far_sem.at[i])

    halo(0).wait_send()
    for i in range(tiles):
        lo, hi = i * B, (i + 1) * B

        @pl.loop(0, heads, unroll=4)
        def _(h):
            query = phi[0, lo:hi, lanes(h)]
            score = lax.dot_general(
                query, phi[1, lo:hi, lanes(h)],
                (((1,), (1,)), ((), ())), preferred_element_type=F32,
            )
            weights = score.astype(BF16) * allow[lo:hi, :]
            got = jnp.dot(weights, phi[2, lo:hi, lanes(h)], preferred_element_type=F32)
            wide = query.astype(F32)
            if i:
                seen = (wide * masks[4, lo:hi, :]).astype(BF16)
                got += jnp.dot(seen, within[i - 1, lanes(h), :], preferred_element_type=F32)
            mix[lo:hi, lanes(h)] = got
            rows_in[0, lo:hi, lanes(h)] = (wide * masks[3, lo:hi, :]).astype(BF16)

        mix_out(i).start()
        far_out(i).start()

    @pl.loop(1, n)
    def _(k):
        back(k).wait_recv()

    state_ref[...] = carried[...]

    for w in (1, 2):
        halo(w).wait_send()

    @pl.loop(1, n)
    def _(k):
        give(k).wait_send()
        back(k).wait_send()

    for i in range(tiles):
        mix_out(i).wait()
        far_out(i).wait()


def finish(mix_ref, far_ref, state_ref, gain_ref, out_ref):
    for h in range(mix_ref.shape[1] // HEAD):
        cols = slice(h * HEAD, (h + 1) * HEAD)
        whole = mix_ref[:, cols] + jnp.dot(
            far_ref[:, cols], state_ref[cols, :], preferred_element_type=F32
        )
        power = jnp.mean(whole * whole, axis=1, keepdims=True)
        out_ref[:, cols] = (whole * lax.rsqrt(power + 1e-6) * gain_ref[:, cols]).astype(BF16)


def per_device(n, query_rows, key_rows, value_rows, lengths, conv_weight, out_gain):
    T, width = query_rows.shape
    anywhere = pl.BlockSpec(memory_space=pl.ANY)
    vmem = pl.BlockSpec(memory_space=pltpu.VMEM)
    tiles = T // B
    mix, far, state = pl.pallas_call(
        functools.partial(kernel, n),
        out_shape=(
            jax.ShapeDtypeStruct((T, width), F32),
            jax.ShapeDtypeStruct((T, width), BF16),
            jax.ShapeDtypeStruct((width, HEAD), BF16),
        ),
        in_specs=[anywhere] * 3 + [vmem] * 2,
        out_specs=(anywhere, anywhere, vmem),
        scratch_shapes=[
            pltpu.VMEM((3, T + PAD, width), BF16),
            pltpu.VMEM((3, T, width), BF16),
            pltpu.VMEM((T, width), F32),
            pltpu.VMEM((5, T, HEAD), F32),
            pltpu.VMEM((T, B), BF16),
            pltpu.VMEM((n, HEAD), F32),
            pltpu.VMEM((tiles - 1, width, HEAD), BF16),
            pltpu.VMEM((width, HEAD), BF16),
            pltpu.VMEM((width, HEAD), BF16),
            pltpu.VMEM((width, HEAD), BF16),
            pltpu.VMEM((width, HEAD), BF16),
            pltpu.SemaphoreType.DMA((3,)),
            pltpu.SemaphoreType.DMA((3,)),
            pltpu.SemaphoreType.DMA((3,)),
            pltpu.SemaphoreType.DMA((2, n)),
            pltpu.SemaphoreType.DMA((2, n)),
            pltpu.SemaphoreType.DMA((tiles,)),
            pltpu.SemaphoreType.DMA((tiles,)),
        ],
        compiler_params=pltpu.CompilerParams(
            collective_id=0, has_side_effects=True, vmem_limit_bytes=62 * 1024 * 1024
        ),
    )(query_rows, key_rows, value_rows, lengths.reshape(1, -1), conv_weight)
    tile = pl.BlockSpec((B, width), lambda i: (i, 0))
    return pl.pallas_call(
        finish,
        grid=(tiles,),
        out_shape=jax.ShapeDtypeStruct((T, width), BF16),
        in_specs=[
            tile,
            tile,
            pl.BlockSpec((width, HEAD), lambda i: (0, 0)),
            pl.BlockSpec((1, width), lambda i: (0, 0)),
        ],
        out_specs=tile,
        compiler_params=pltpu.CompilerParams(vmem_limit_bytes=62 * 1024 * 1024),
    )(mix, far, state, out_gain.reshape(1, -1))


def solution(mesh):
    return jax.shard_map(
        functools.partial(per_device, mesh.shape["ctx"]),
        mesh=mesh,
        in_specs=(
            P(("dp", "ctx"), None),
            P(("dp", "ctx"), None),
            P(("dp", "ctx"), None),
            P("dp"),
            P(),
            P(),
        ),
        out_specs=P(("dp", "ctx"), None),
        check_vma=False,
    )
```

```python
import functools

import jax
import jax.numpy as jnp
from jax import lax
from jax.experimental import pallas as pl
from jax.experimental.pallas import tpu as pltpu
from jax.sharding import PartitionSpec as P

HEAD = 128
PAD = 128
EDGE = 16
B = 256
MESH = pl.DeviceIdType.MESH
F32 = jnp.float32
BF16 = jnp.bfloat16


def lanes(head):
    return pl.ds(pl.multiple_of(head * HEAD, HEAD), HEAD)


def iota(shape, dim):
    return lax.broadcasted_iota(jnp.int32, shape, dim).astype(F32)


def kernel(
    n, q_hbm, k_hbm, v_hbm, len_ref, cw_ref, mix_hbm, far_hbm, state_ref,
    rows_in, phi, mix, masks, shifts, allow, keeps, within, tail, gathered, scanned, carried,
    load_sem, halo_send, halo_recv, send_sem, recv_sem, mix_sem, far_sem,
):
    me = lax.axis_index("ctx")
    T, width = q_hbm.shape
    heads = width // HEAD
    R = width // n
    per = n // heads
    ndoc = len_ref.shape[1]
    tiles = T // B
    inputs = (q_hbm, k_hbm, v_hbm)

    def load(w):
        return pltpu.make_async_copy(inputs[w], rows_in.at[w, pl.ds(PAD, T)], load_sem.at[w])

    for w in (1, 2, 0):
        load(w).start()

    barrier = pltpu.get_barrier_semaphore()

    @pl.loop(1, n)
    def _(k):
        pl.semaphore_signal(
            barrier, inc=1, device_id={"ctx": lax.rem(me + k, n)}, device_id_type=MESH
        )

    sub = lax.broadcasted_iota(jnp.int32, (ndoc, ndoc), 0)
    lan = lax.broadcasted_iota(jnp.int32, (ndoc, ndoc), 1)
    lens = len_ref[...].astype(F32)
    col = jnp.sum(jnp.where(lan < sub, lens, 0.0), axis=1, keepdims=True)
    starts = jnp.sum(jnp.where(lan == sub, col, 0.0), axis=0, keepdims=True)
    offset = (me * T).astype(F32)

    first = iota((n, ndoc), 0) * T
    inside = (starts >= first) & (starts < first + T)
    hit = jnp.max(jnp.where(inside, 1.0, 0.0), axis=1, keepdims=True)
    keeps[...] = jnp.broadcast_to(1.0 - hit, (n, HEAD))

    MC = 128
    for c in range(T // MC):
        r0 = c * MC
        local = iota((MC, 1), 0) + r0
        pos = local + offset
        mine = jnp.max(jnp.where(starts <= pos, starts, -1.0), axis=1, keepdims=True)
        depth = jnp.broadcast_to(pos - mine, (MC, HEAD))
        rows = pl.ds(r0, MC)
        wide = jnp.concatenate([depth, depth], axis=1)
        away = iota((MC, 2 * HEAD), 0) + PAD - iota((MC, 2 * HEAD), 1)
        for j in range(1, 4):
            here = (away == j) & (wide >= j)
            shifts[c, (j - 1) * MC : j * MC, :] = jnp.where(here, 1.0, 0.0).astype(BF16)
        masks[0, rows, :] = (depth > local).astype(F32)
        opening = (r0 // B) * B
        masks[1, rows, :] = (depth > local - opening).astype(F32)
        for piece in range(B // HEAD):
            gap = local - (iota((MC, HEAD), 1) + (opening + piece * HEAD))
            ok = (gap >= 0.0) & (gap <= depth)
            allow[rows, piece * HEAD : (piece + 1) * HEAD] = jnp.where(ok, 1.0, 0.0).astype(BF16)

    def last_start(c):
        end = offset + ((c + 1) * B - 1)
        return jnp.max(jnp.where(starts <= end, starts, -1.0), axis=1, keepdims=True)

    lasts = [last_start(c) - offset for c in range(tiles)]
    goes_on = [(lasts[c] < c * B).astype(F32) for c in range(tiles)]

    nxt = lax.rem(me + 1, n)

    def halo(w):
        return pltpu.make_async_remote_copy(
            src_ref=inputs[w].at[pl.ds(T - EDGE, EDGE)],
            dst_ref=rows_in.at[w, pl.ds(PAD - EDGE, EDGE)],
            send_sem=halo_send.at[w],
            recv_sem=halo_recv.at[w],
            device_id={"ctx": nxt},
            device_id_type=MESH,
        )

    for w in range(3):
        rows_in[w, 0 : PAD - EDGE, :] = jnp.zeros((PAD - EDGE, width), BF16)

    pl.semaphore_wait(barrier, n - 1)
    for w in (1, 2, 0):
        halo(w).start()

    C = 128
    chunks = T // C

    def conv(w, pair, c):
        rows = pl.ds(c * C, C)
        cols = pl.ds(pl.multiple_of(pair * 2 * HEAD, 2 * HEAD), 2 * HEAD)
        moved = jnp.dot(
            shifts[c], rows_in[w, pl.ds(c * C, C + PAD), cols], preferred_element_type=F32
        )
        scale = 1.0 if w == 2 else 0.5
        now = rows_in[w, pl.ds(c * C + PAD, C), cols].astype(F32)
        acc = now * (cw_ref[w, 0:1, cols] * scale)
        for j in range(1, 4):
            acc += moved[(j - 1) * C : j * C] * (cw_ref[w, j : j + 1, cols] * scale)
        if w < 2:
            acc = acc + acc * jnp.tanh(acc)
        phi[w, rows, cols] = acc.astype(BF16)

    def slice_rows(d):
        return pl.ds(pl.multiple_of(d * R, R), R)

    def give(k):
        to = lax.rem(me + k, n)
        return pltpu.make_async_remote_copy(
            src_ref=tail.at[slice_rows(to)],
            dst_ref=gathered.at[slice_rows(me)],
            send_sem=send_sem.at[0, k],
            recv_sem=recv_sem.at[0, k],
            device_id={"ctx": to},
            device_id_type=MESH,
        )

    def back(k):
        to = lax.rem(me + k, n)
        return pltpu.make_async_remote_copy(
            src_ref=scanned.at[slice_rows(to)],
            dst_ref=carried.at[slice_rows(me)],
            send_sem=send_sem.at[1, k],
            recv_sem=recv_sem.at[1, k],
            device_id={"ctx": to},
            device_id_type=MESH,
        )

    def order(i):
        return lax.rem(me // (2 * per) + 1 + i, heads // 2)

    EARLY = 1
    load(1).wait()
    load(2).wait()

    @pl.loop(0, EARLY)
    def _(i):
        for c in range(chunks - 1, 0, -1):
            conv(1, order(i), c)
            conv(2, order(i), c)

    halo(1).wait_recv()
    halo(2).wait_recv()

    @pl.loop(0, heads // 2)
    def _(i):
        pair = order(i)

        @pl.when(i >= EARLY)
        def _():
            for c in range(chunks - 1, 0, -1):
                conv(1, pair, c)
                conv(2, pair, c)

        conv(1, pair, 0)
        conv(2, pair, 0)
        for one in range(2):
            h = pair * 2 + one
            state = None
            for c in range(tiles):
                rows = slice(c * B, (c + 1) * B)
                live = (iota((B, HEAD), 0) + c * B) >= lasts[c]
                key = jnp.where(live, phi[1, rows, lanes(h)].astype(F32), 0.0).astype(BF16)
                own = lax.dot_general(
                    key, phi[2, rows, lanes(h)], (((0,), (0,)), ((), ())),
                    preferred_element_type=F32,
                )
                state = own if state is None else state * goes_on[c] + own
                if c < tiles - 1:
                    within[c, lanes(h), :] = state.astype(BF16)
            tail[lanes(h), :] = state.astype(BF16)

        @pl.loop(0, 2 * per)
        def _(j):
            k = lax.rem(pair * 2 * per + j - me + n, n)

            @pl.when(k != 0)
            def _():
                give(k).start()

    gathered[slice_rows(me), :] = tail[slice_rows(me), :]

    load(0).wait()
    halo(0).wait_recv()

    def conv_q(h):
        for c in range(chunks):
            conv(0, h, c)

    pl.loop(0, EARLY)(conv_q)

    @pl.loop(1, n)
    def _(k):
        give(k).wait_recv()

    def step(b, state):
        scanned[slice_rows(b), :] = state.astype(BF16)
        return state * keeps[pl.ds(b, 1), :] + gathered[slice_rows(b), :].astype(F32)

    lax.fori_loop(0, n, step, jnp.zeros((R, HEAD), F32), unroll=4)

    @pl.loop(1, n)
    def _(k):
        back(k).start()

    carried[slice_rows(me), :] = scanned[slice_rows(me), :]

    pl.loop(EARLY, heads // 2)(conv_q)

    def mix_out(i):
        rows = pl.ds(i * B, B)
        return pltpu.make_async_copy(mix.at[rows], mix_hbm.at[rows], mix_sem.at[i])

    def far_out(i):
        rows = pl.ds(i * B, B)
        return pltpu.make_async_copy(rows_in.at[0, rows], far_hbm.at[rows], far_sem.at[i])

    halo(0).wait_send()
    for i in range(tiles):
        lo, hi = i * B, (i + 1) * B

        @pl.loop(0, heads, unroll=4)
        def _(h):
            query = phi[0, lo:hi, lanes(h)]
            score = lax.dot_general(
                query, phi[1, lo:hi, lanes(h)],
                (((1,), (1,)), ((), ())), preferred_element_type=F32,
            )
            weights = score.astype(BF16) * allow[lo:hi, :]
            got = jnp.dot(weights, phi[2, lo:hi, lanes(h)], preferred_element_type=F32)
            wide = query.astype(F32)
            if i:
                seen = (wide * masks[1, lo:hi, :]).astype(BF16)
                got += jnp.dot(seen, within[i - 1, lanes(h), :], preferred_element_type=F32)
            mix[lo:hi, lanes(h)] = got
            rows_in[0, lo:hi, lanes(h)] = (wide * masks[0, lo:hi, :]).astype(BF16)

        mix_out(i).start()
        far_out(i).start()

    @pl.loop(1, n)
    def _(k):
        back(k).wait_recv()

    state_ref[...] = carried[...]

    for w in (1, 2):
        halo(w).wait_send()

    @pl.loop(1, n)
    def _(k):
        give(k).wait_send()
        back(k).wait_send()

    for i in range(tiles):
        mix_out(i).wait()
        far_out(i).wait()


def finish(mix_ref, far_ref, state_ref, gain_ref, out_ref):
    average = jnp.full((HEAD, HEAD), 1.0 / HEAD, BF16)
    for h in range(mix_ref.shape[1] // HEAD):
        cols = slice(h * HEAD, (h + 1) * HEAD)
        whole = mix_ref[:, cols] + jnp.dot(
            far_ref[:, cols], state_ref[cols, :], preferred_element_type=F32
        )
        square = (whole * whole).astype(BF16)
        power = jnp.dot(square, average, preferred_element_type=F32)
        out_ref[:, cols] = (whole * lax.rsqrt(power + 1e-6) * gain_ref[:, cols]).astype(BF16)


def per_device(n, query_rows, key_rows, value_rows, lengths, conv_weight, out_gain):
    T, width = query_rows.shape
    anywhere = pl.BlockSpec(memory_space=pl.ANY)
    vmem = pl.BlockSpec(memory_space=pltpu.VMEM)
    tiles = T // B
    mix, far, state = pl.pallas_call(
        functools.partial(kernel, n),
        out_shape=(
            jax.ShapeDtypeStruct((T, width), F32),
            jax.ShapeDtypeStruct((T, width), BF16),
            jax.ShapeDtypeStruct((width, HEAD), BF16),
        ),
        in_specs=[anywhere] * 3 + [vmem] * 2,
        out_specs=(anywhere, anywhere, vmem),
        scratch_shapes=[
            pltpu.VMEM((3, T + PAD, width), BF16),
            pltpu.VMEM((3, T, width), BF16),
            pltpu.VMEM((T, width), F32),
            pltpu.VMEM((2, T, HEAD), F32),
            pltpu.VMEM((T // 128, 384, 2 * HEAD), BF16),
            pltpu.VMEM((T, B), BF16),
            pltpu.VMEM((n, HEAD), F32),
            pltpu.VMEM((tiles - 1, width, HEAD), BF16),
            pltpu.VMEM((width, HEAD), BF16),
            pltpu.VMEM((width, HEAD), BF16),
            pltpu.VMEM((width, HEAD), BF16),
            pltpu.VMEM((width, HEAD), BF16),
            pltpu.SemaphoreType.DMA((3,)),
            pltpu.SemaphoreType.DMA((3,)),
            pltpu.SemaphoreType.DMA((3,)),
            pltpu.SemaphoreType.DMA((2, n)),
            pltpu.SemaphoreType.DMA((2, n)),
            pltpu.SemaphoreType.DMA((tiles,)),
            pltpu.SemaphoreType.DMA((tiles,)),
        ],
        compiler_params=pltpu.CompilerParams(
            collective_id=0, has_side_effects=True, vmem_limit_bytes=62 * 1024 * 1024
        ),
    )(query_rows, key_rows, value_rows, lengths.reshape(1, -1), conv_weight)
    tile = pl.BlockSpec((B, width), lambda i: (i, 0))
    return pl.pallas_call(
        finish,
        grid=(tiles,),
        out_shape=jax.ShapeDtypeStruct((T, width), BF16),
        in_specs=[
            tile,
            tile,
            pl.BlockSpec((width, HEAD), lambda i: (0, 0)),
            pl.BlockSpec((1, width), lambda i: (0, 0)),
        ],
        out_specs=tile,
        compiler_params=pltpu.CompilerParams(vmem_limit_bytes=62 * 1024 * 1024),
    )(mix, far, state, out_gain.reshape(1, -1))


def solution(mesh):
    return jax.shard_map(
        functools.partial(per_device, mesh.shape["ctx"]),
        mesh=mesh,
        in_specs=(
            P(("dp", "ctx"), None),
            P(("dp", "ctx"), None),
            P(("dp", "ctx"), None),
            P("dp"),
            P(),
            P(),
        ),
        out_specs=P(("dp", "ctx"), None),
        check_vma=False,
    )
```

```python
import functools

import jax
import jax.numpy as jnp
from jax import lax
from jax.experimental import pallas as pl
from jax.experimental.pallas import tpu as pltpu
from jax.sharding import PartitionSpec as P

HEAD = 128
PAD = 128
EDGE = 16
B = 256
MESH = pl.DeviceIdType.MESH
F32 = jnp.float32
BF16 = jnp.bfloat16


def lanes(head):
    return pl.ds(pl.multiple_of(head * HEAD, HEAD), HEAD)


def iota(shape, dim):
    return lax.broadcasted_iota(jnp.int32, shape, dim).astype(F32)


def kernel(
    n, q_hbm, k_hbm, v_hbm, len_ref, cw_ref, mix_hbm, far_hbm, state_ref,
    rows_in, phi, mix, masks, shifts, allow, keeps, within, tail, gathered, scanned, carried,
    load_sem, halo_send, halo_recv, send_sem, recv_sem, mix_sem, far_sem,
):
    me = lax.axis_index("ctx")
    T, width = q_hbm.shape
    heads = width // HEAD
    R = width // n
    per = n // heads
    ndoc = len_ref.shape[1]
    tiles = T // B
    inputs = (q_hbm, k_hbm, v_hbm)

    def load(w):
        return pltpu.make_async_copy(inputs[w], rows_in.at[w, pl.ds(PAD, T)], load_sem.at[w])

    for w in (1, 2, 0):
        load(w).start()

    barrier = pltpu.get_barrier_semaphore()

    @pl.loop(1, n)
    def _(k):
        pl.semaphore_signal(
            barrier, inc=1, device_id={"ctx": lax.rem(me + k, n)}, device_id_type=MESH
        )

    sub = lax.broadcasted_iota(jnp.int32, (ndoc, ndoc), 0)
    lan = lax.broadcasted_iota(jnp.int32, (ndoc, ndoc), 1)
    lens = len_ref[...].astype(F32)
    col = jnp.sum(jnp.where(lan < sub, lens, 0.0), axis=1, keepdims=True)
    starts = jnp.sum(jnp.where(lan == sub, col, 0.0), axis=0, keepdims=True)
    offset = (me * T).astype(F32)

    first = iota((n, ndoc), 0) * T
    inside = (starts >= first) & (starts < first + T)
    hit = jnp.max(jnp.where(inside, 1.0, 0.0), axis=1, keepdims=True)
    keeps[...] = jnp.broadcast_to(1.0 - hit, (n, HEAD))

    MC = 128
    for c in range(T // MC):
        r0 = c * MC
        local = iota((MC, 1), 0) + r0
        pos = local + offset
        mine = jnp.max(jnp.where(starts <= pos, starts, -1.0), axis=1, keepdims=True)
        depth = jnp.broadcast_to(pos - mine, (MC, HEAD))
        rows = pl.ds(r0, MC)
        wide = jnp.concatenate([depth, depth], axis=1)
        away = iota((MC, 2 * HEAD), 0) + PAD - iota((MC, 2 * HEAD), 1)
        for j in range(1, 4):
            here = (away == j) & (wide >= j)
            shifts[c, (j - 1) * MC : j * MC, :] = jnp.where(here, 1.0, 0.0).astype(BF16)
        masks[0, rows, :] = (depth > local).astype(F32)
        opening = (r0 // B) * B
        masks[1, rows, :] = (depth > local - opening).astype(F32)
        for piece in range(B // HEAD):
            gap = local - (iota((MC, HEAD), 1) + (opening + piece * HEAD))
            ok = (gap >= 0.0) & (gap <= depth)
            allow[rows, piece * HEAD : (piece + 1) * HEAD] = jnp.where(ok, 1.0, 0.0).astype(BF16)

    def last_start(c):
        end = offset + ((c + 1) * B - 1)
        return jnp.max(jnp.where(starts <= end, starts, -1.0), axis=1, keepdims=True)

    lasts = [last_start(c) - offset for c in range(tiles)]
    goes_on = [(lasts[c] < c * B).astype(F32) for c in range(tiles)]

    nxt = lax.rem(me + 1, n)

    def halo(w):
        return pltpu.make_async_remote_copy(
            src_ref=inputs[w].at[pl.ds(T - EDGE, EDGE)],
            dst_ref=rows_in.at[w, pl.ds(PAD - EDGE, EDGE)],
            send_sem=halo_send.at[w],
            recv_sem=halo_recv.at[w],
            device_id={"ctx": nxt},
            device_id_type=MESH,
        )

    for w in range(3):
        rows_in[w, 0 : PAD - EDGE, :] = jnp.zeros((PAD - EDGE, width), BF16)

    pl.semaphore_wait(barrier, n - 1)
    for w in (1, 2, 0):
        halo(w).start()

    C = 128
    chunks = T // C

    def conv(w, pair, c):
        rows = pl.ds(c * C, C)
        cols = pl.ds(pl.multiple_of(pair * 2 * HEAD, 2 * HEAD), 2 * HEAD)
        moved = jnp.dot(
            shifts[c], rows_in[w, pl.ds(c * C, C + PAD), cols], preferred_element_type=F32
        )
        scale = 1.0 if w == 2 else 0.5
        now = rows_in[w, pl.ds(c * C + PAD, C), cols].astype(F32)
        acc = now * (cw_ref[w, 0:1, cols] * scale)
        for j in range(1, 4):
            acc += moved[(j - 1) * C : j * C] * (cw_ref[w, j : j + 1, cols] * scale)
        if w < 2:
            acc = acc + acc * jnp.tanh(acc)
        phi[w, rows, cols] = acc.astype(BF16)

    def slice_rows(d):
        return pl.ds(pl.multiple_of(d * R, R), R)

    def give(k):
        to = lax.rem(me + k, n)
        return pltpu.make_async_remote_copy(
            src_ref=tail.at[slice_rows(to)],
            dst_ref=gathered.at[slice_rows(me)],
            send_sem=send_sem.at[0, k],
            recv_sem=recv_sem.at[0, k],
            device_id={"ctx": to},
            device_id_type=MESH,
        )

    def back(k):
        to = lax.rem(me + k, n)
        return pltpu.make_async_remote_copy(
            src_ref=scanned.at[slice_rows(to)],
            dst_ref=carried.at[slice_rows(me)],
            send_sem=send_sem.at[1, k],
            recv_sem=recv_sem.at[1, k],
            device_id={"ctx": to},
            device_id_type=MESH,
        )

    def order(i):
        return lax.rem(me // (2 * per) + 1 + i, heads // 2)

    EARLY = 1
    load(1).wait()
    load(2).wait()

    @pl.loop(0, EARLY)
    def _(i):
        for c in range(chunks - 1, 0, -1):
            conv(1, order(i), c)
            conv(2, order(i), c)

    halo(1).wait_recv()
    halo(2).wait_recv()

    @pl.loop(0, heads // 2)
    def _(i):
        pair = order(i)

        @pl.when(i >= EARLY)
        def _():
            for c in range(chunks - 1, 0, -1):
                conv(1, pair, c)
                conv(2, pair, c)

        conv(1, pair, 0)
        conv(2, pair, 0)
        for one in range(2):
            h = pair * 2 + one
            state = None
            for c in range(tiles):
                rows = slice(c * B, (c + 1) * B)
                live = (iota((B, HEAD), 0) + c * B) >= lasts[c]
                key = jnp.where(live, phi[1, rows, lanes(h)].astype(F32), 0.0).astype(BF16)
                own = lax.dot_general(
                    key, phi[2, rows, lanes(h)], (((0,), (0,)), ((), ())),
                    preferred_element_type=F32,
                )
                state = own if state is None else state * goes_on[c] + own
                if c < tiles - 1:
                    within[c, lanes(h), :] = state.astype(BF16)
            tail[lanes(h), :] = state.astype(BF16)

        @pl.loop(0, 2 * per)
        def _(j):
            k = lax.rem(pair * 2 * per + j - me + n, n)

            @pl.when(k != 0)
            def _():
                give(k).start()

    gathered[slice_rows(me), :] = tail[slice_rows(me), :]

    load(0).wait()
    halo(0).wait_recv()

    def conv_q(h):
        for c in range(chunks):
            conv(0, h, c)

    pl.loop(0, EARLY)(conv_q)

    @pl.loop(1, n)
    def _(k):
        give(k).wait_recv()

    def step(b, state):
        scanned[slice_rows(b), :] = state.astype(BF16)
        return state * keeps[pl.ds(b, 1), :] + gathered[slice_rows(b), :].astype(F32)

    lax.fori_loop(0, n, step, jnp.zeros((R, HEAD), F32), unroll=4)

    @pl.loop(1, n)
    def _(k):
        back(k).start()

    carried[slice_rows(me), :] = scanned[slice_rows(me), :]

    pl.loop(EARLY, heads // 2)(conv_q)

    def mix_out(i):
        rows = pl.ds(i * B, B)
        return pltpu.make_async_copy(mix.at[rows], mix_hbm.at[rows], mix_sem.at[i])

    def far_out(i):
        rows = pl.ds(i * B, B)
        return pltpu.make_async_copy(rows_in.at[0, rows], far_hbm.at[rows], far_sem.at[i])

    halo(0).wait_send()
    for i in range(tiles):
        lo, hi = i * B, (i + 1) * B

        @pl.loop(0, heads, unroll=4)
        def _(h):
            query = phi[0, lo:hi, lanes(h)]
            score = lax.dot_general(
                query, phi[1, lo:hi, lanes(h)],
                (((1,), (1,)), ((), ())), preferred_element_type=F32,
            )
            weights = score.astype(BF16) * allow[lo:hi, :]
            got = jnp.dot(weights, phi[2, lo:hi, lanes(h)], preferred_element_type=F32)
            wide = query.astype(F32)
            if i:
                seen = (wide * masks[1, lo:hi, :]).astype(BF16)
                got += jnp.dot(seen, within[i - 1, lanes(h), :], preferred_element_type=F32)
            mix[lo:hi, lanes(h)] = got.astype(BF16)
            rows_in[0, lo:hi, lanes(h)] = (wide * masks[0, lo:hi, :]).astype(BF16)

        mix_out(i).start()
        far_out(i).start()

    @pl.loop(1, n)
    def _(k):
        back(k).wait_recv()

    state_ref[...] = carried[...]

    for w in (1, 2):
        halo(w).wait_send()

    @pl.loop(1, n)
    def _(k):
        give(k).wait_send()
        back(k).wait_send()

    for i in range(tiles):
        mix_out(i).wait()
        far_out(i).wait()


def finish(mix_ref, far_ref, state_ref, gain_ref, out_ref):
    average = jnp.full((HEAD, HEAD), 1.0 / HEAD, BF16)
    for h in range(mix_ref.shape[1] // HEAD):
        cols = slice(h * HEAD, (h + 1) * HEAD)
        whole = mix_ref[:, cols].astype(F32) + jnp.dot(
            far_ref[:, cols], state_ref[cols, :], preferred_element_type=F32
        )
        square = (whole * whole).astype(BF16)
        power = jnp.dot(square, average, preferred_element_type=F32)
        out_ref[:, cols] = (whole * lax.rsqrt(power + 1e-6) * gain_ref[:, cols]).astype(BF16)


def per_device(n, query_rows, key_rows, value_rows, lengths, conv_weight, out_gain):
    T, width = query_rows.shape
    anywhere = pl.BlockSpec(memory_space=pl.ANY)
    vmem = pl.BlockSpec(memory_space=pltpu.VMEM)
    tiles = T // B
    mix, far, state = pl.pallas_call(
        functools.partial(kernel, n),
        out_shape=(
            jax.ShapeDtypeStruct((T, width), BF16),
            jax.ShapeDtypeStruct((T, width), BF16),
            jax.ShapeDtypeStruct((width, HEAD), BF16),
        ),
        in_specs=[anywhere] * 3 + [vmem] * 2,
        out_specs=(anywhere, anywhere, vmem),
        scratch_shapes=[
            pltpu.VMEM((3, T + PAD, width), BF16),
            pltpu.VMEM((3, T, width), BF16),
            pltpu.VMEM((T, width), BF16),
            pltpu.VMEM((2, T, HEAD), F32),
            pltpu.VMEM((T // 128, 384, 2 * HEAD), BF16),
            pltpu.VMEM((T, B), BF16),
            pltpu.VMEM((n, HEAD), F32),
            pltpu.VMEM((tiles - 1, width, HEAD), BF16),
            pltpu.VMEM((width, HEAD), BF16),
            pltpu.VMEM((width, HEAD), BF16),
            pltpu.VMEM((width, HEAD), BF16),
            pltpu.VMEM((width, HEAD), BF16),
            pltpu.SemaphoreType.DMA((3,)),
            pltpu.SemaphoreType.DMA((3,)),
            pltpu.SemaphoreType.DMA((3,)),
            pltpu.SemaphoreType.DMA((2, n)),
            pltpu.SemaphoreType.DMA((2, n)),
            pltpu.SemaphoreType.DMA((tiles,)),
            pltpu.SemaphoreType.DMA((tiles,)),
        ],
        compiler_params=pltpu.CompilerParams(
            collective_id=0, has_side_effects=True, vmem_limit_bytes=62 * 1024 * 1024
        ),
    )(query_rows, key_rows, value_rows, lengths.reshape(1, -1), conv_weight)
    tile = pl.BlockSpec((B, width), lambda i: (i, 0))
    return pl.pallas_call(
        finish,
        grid=(tiles,),
        out_shape=jax.ShapeDtypeStruct((T, width), BF16),
        in_specs=[
            tile,
            tile,
            pl.BlockSpec((width, HEAD), lambda i: (0, 0)),
            pl.BlockSpec((1, width), lambda i: (0, 0)),
        ],
        out_specs=tile,
        compiler_params=pltpu.CompilerParams(vmem_limit_bytes=62 * 1024 * 1024),
    )(mix, far, state, out_gain.reshape(1, -1))


def solution(mesh):
    return jax.shard_map(
        functools.partial(per_device, mesh.shape["ctx"]),
        mesh=mesh,
        in_specs=(
            P(("dp", "ctx"), None),
            P(("dp", "ctx"), None),
            P(("dp", "ctx"), None),
            P("dp"),
            P(),
            P(),
        ),
        out_specs=P(("dp", "ctx"), None),
        check_vma=False,
    )
```
